32 devices in a mesh: ctx: 32 (over z, y, x, core), vocab: 1.
Axes of the slice: x: 2, y: 2, z: 4, core: 2. Of those that a mesh axis runs over, the one named last changes fastest.
Arguments:
- hidden_states: bfloat16 [8192, 8192], P('ctx'), may hold values from -24 to 24
- master: float32 [128, 8192], P(('vocab', 'ctx')), may hold values from -1 to 1
- moment: float32 [128, 8192], P(('vocab', 'ctx')), may hold values from -6 to 6
- second: float32 [128, 8192], P(('vocab', 'ctx')), may hold values from 0.05 to 5
- targets: int32 [8192], P('ctx'), may hold values from 0 to 255, as said below
- loss_mask: int32 [8192], P('ctx'), may hold values from 0 to 1, as said below
- prior_lse: float32 [8192], P('ctx'), may hold values from 6 to 9
- prior_target: float32 [8192], P('ctx'), may hold values from -5 to 5
- span_order: int32 [64], replicated, may hold values from 0 to 63, as said below
Outputs:
- token_loss: float32 [8192], P('ctx')
- mean_loss: float32 [], replicated
- hidden_grad: bfloat16 [8192, 8192], P('ctx', 'vocab')
- new_master: float32 [128, 8192], P(('vocab', 'ctx'))
- new_moment: float32 [128, 8192], P(('vocab', 'ctx'))
- new_second: float32 [128, 8192], P(('vocab', 'ctx'))
The draws below stay inside these ranges and needn't reach their ends.
Inputs may be any that keep to these rules, and one draw needn't show every extreme that they name: `targets`: ids of 128 and more fall in this block, id minus 128 naming its row; smaller ids lie in earlier blocks. `loss_mask`: 1 on a leading run of the slab's positions and 0 after it; at least 2048 ones. `span_order`: each span number once.
All inputs are finite; a program needn't handle non-finite values.
Results may differ from the reference program's by a relative error of at most 0.0085.
Values may be sent and summed in bfloat16 or wider, within the bound.
A program may use at most 128 MiB of HBM per device.

```python
import math
import jax
import jax.numpy as jnp
from jax import lax

D = 8192
SPAN = 128
SPANS = 64
TOKENS = 8192
VBLOCK = 128
N_VOCAB = 1


hit_rows = 16


per_row = 4


def head_table(key):
    return jnp.clip(jax.random.normal(key, (VBLOCK, D), jnp.float32), -6.0, 6.0) * D ** (-0.5)


def layout_order(key):
    return jax.random.permutation(jax.random.fold_in(key, 31), SPANS).astype(jnp.int32)


def target_ids(key):
    far_ids = jax.random.randint(jax.random.fold_in(key, 41), (TOKENS,), 0, VBLOCK, dtype=jnp.int32)
    far_ids = far_ids.at[TOKENS - 1].set(0)
    stride = VBLOCK // hit_rows
    jitter = jax.random.randint(jax.random.fold_in(key, 42), (hit_rows,), 0, stride, dtype=jnp.int32)
    jitter = jitter.at[0].set(0)
    block_rows = VBLOCK - 1 - jnp.arange(hit_rows, dtype=jnp.int32) * stride - jitter
    spots = jax.random.permutation(jax.random.fold_in(key, 43), TOKENS // 4)[:hit_rows * per_row].astype(jnp.int32)
    block_ids = jnp.repeat(block_rows, per_row) + VBLOCK
    return far_ids.at[spots].set(block_ids.astype(jnp.int32))


def draw_targets(key, part):
    return target_ids(key)


def draw_span_order(key, part):
    return layout_order(key)


def draw_master(key, part):
    return head_table(jax.random.fold_in(key, 11))


def draw_hidden_states(key, part):
    order = layout_order(key)
    row_pos = (order[:, None] * SPAN + jnp.arange(SPAN, dtype=jnp.int32)[None, :]).reshape(-1)
    row_targets = target_ids(key)[row_pos]
    cluster = jnp.clip(jax.random.normal(jax.random.fold_in(key, 51), (2 * VBLOCK, D), jnp.float32), -6.0, 6.0)
    shared = cluster[row_targets]
    base = jnp.clip(jax.random.normal(jax.random.fold_in(key, 1), (TOKENS, D), jnp.float32), -6.0, 6.0)
    base = jnp.clip(base + shared, -24.0, 24.0)
    return base.astype(jnp.bfloat16)


def draw_loss_mask(key, part):
    valid = jax.random.randint(key, (), TOKENS // 4, TOKENS + 1)
    return (jnp.arange(TOKENS, dtype=jnp.int32) < valid).astype(jnp.int32)


def shard_levels(stream_key, shape, shards, low, high):
    def one(axis_at, blocks):
        heights = jax.random.uniform(jax.random.fold_in(jax.random.fold_in(stream_key, 6), axis_at), (blocks,), jnp.float32, low / len(shards), high / len(shards))
        return jnp.repeat(jnp.exp(heights), shape[axis_at] // blocks).reshape((-1,) + (1,) * (len(shape) - axis_at - 1))

    gain = one(*shards[0])
    for cut in shards[1:]:
        gain = gain * one(*cut)
    return gain


def scatter_about(key, dims, spread, limit, shards=(), kind=jnp.bfloat16):
    entries = spread * jax.random.normal(key, dims, jnp.float32)
    if shards:
        entries = entries * shard_levels(key, dims, shards, -0.22, 0.18)
    return jnp.clip(entries, -limit, limit).astype(kind)


def setup_inputs(seed: int = 0) -> dict:
    splits = jax.random.split(jax.random.key(seed), 10)
    hidden_states = draw_hidden_states(jax.random.fold_in(splits[9], 71), 0)
    master = draw_master(jax.random.fold_in(splits[9], 71), 0)
    moment = scatter_about(splits[2], (VBLOCK, D), 1.0, 6.0, ((0, 32),), jnp.float32)
    second = jnp.clip(jnp.exp(math.log(5.0) - 4.6051702 * jax.random.uniform(splits[3], (VBLOCK, D), jnp.float32) ** shard_levels(splits[3], (VBLOCK, D), ((0, 32),), -0.2, 0.2)), 0.05, 5.0)
    targets = draw_targets(jax.random.fold_in(splits[9], 71), 0)
    loss_mask = draw_loss_mask(jax.random.fold_in(splits[9], 71), 0)
    prior_lse = jnp.clip(6.0 + 3.0 * jax.random.uniform(splits[6], (TOKENS,), jnp.float32) ** shard_levels(splits[6], (TOKENS,), ((0, 32),), -0.2, 0.2), 6.0, 9.0)
    prior_target = scatter_about(splits[7], (TOKENS,), 1.0, 5.0, ((0, 32),), jnp.float32)
    span_order = draw_span_order(jax.random.fold_in(splits[9], 71), 0)
    return {"hidden_states": hidden_states, "master": master, "moment": moment, "second": second, "targets": targets, "loss_mask": loss_mask, "prior_lse": prior_lse, "prior_target": prior_target, "span_order": span_order}


loss_scale = 1048576.0
clip_norm = 0.004
beta_one = 0.9
beta_two = 0.95
learn_rate = 0.001
weight_decay = 0.1
adam_eps = 1e-08

def reference(hidden_states, master, moment, second, targets, loss_mask, prior_lse, prior_target, span_order):
    row_pos = (span_order[:, None] * SPAN + jnp.arange(SPAN, dtype=jnp.int32)[None, :]).reshape(-1).astype(jnp.int32)
    tgt_rows = targets[row_pos]
    mask_rows = loss_mask[row_pos].astype(jnp.float32)
    prior_rows = prior_lse[row_pos]
    outside = prior_target[row_pos]
    head_rows = master.astype(jnp.bfloat16)
    logits = jnp.dot(hidden_states, head_rows.T, preferred_element_type=jnp.float32)
    columns = jnp.arange(VBLOCK, dtype=jnp.int32)
    onehot = (columns[None, :] == (tgt_rows - VBLOCK)[:, None]).astype(jnp.float32)
    inside = lax.optimization_barrier(jnp.sum(logits * onehot, axis=1))
    target_logit = jnp.where(tgt_rows >= VBLOCK, inside, outside)
    top_value = jnp.maximum(prior_rows, lax.optimization_barrier(jnp.max(logits, axis=1)))
    log_total = top_value + jnp.log(jnp.exp(prior_rows - top_value) + lax.optimization_barrier(jnp.sum(jnp.exp(logits - top_value[:, None]), axis=1)))
    token_count = jnp.sum(loss_mask.astype(jnp.float32))
    loss_rows = mask_rows * (log_total - target_logit)
    token_loss = jnp.zeros((TOKENS,), jnp.float32).at[row_pos].set(loss_rows)
    mean_loss = jnp.sum(loss_rows) / token_count
    grad_scale = loss_scale / token_count
    dlogits = (mask_rows[:, None] * (jnp.exp(logits - log_total[:, None]) - onehot) * grad_scale).astype(jnp.bfloat16)
    row_grad = jnp.dot(dlogits.T, hidden_states, preferred_element_type=jnp.float32)
    quarter = VBLOCK // N_VOCAB
    hidden_sum = jnp.zeros((TOKENS, D), jnp.float32)
    for part_index in range(N_VOCAB):
        lower = part_index * quarter
        partial_value = jnp.dot(dlogits[:, lower:lower + quarter], head_rows[lower:lower + quarter], preferred_element_type=jnp.float32).astype(jnp.bfloat16)
        partial_value = lax.optimization_barrier(partial_value)
        hidden_sum = hidden_sum + partial_value.astype(jnp.float32)
    hidden_grad = hidden_sum.astype(jnp.bfloat16)
    square_sum = jnp.sum(row_grad * row_grad)
    norm_value = jnp.sqrt(square_sum) / loss_scale
    clip_factor = jnp.minimum(1.0, clip_norm / (norm_value + 1e-06))
    clipped = row_grad * clip_factor
    new_moment = beta_one * moment + (1.0 - beta_one) * clipped
    new_second = beta_two * second + (1.0 - beta_two) * clipped * clipped
    new_master = master - learn_rate * (new_moment / (jnp.sqrt(new_second) + adam_eps) + weight_decay * master)
    return (token_loss, mean_loss, hidden_grad, new_master, new_moment, new_second)
```

```python
import functools

import jax
import jax.numpy as jnp
from jax import lax
from jax.experimental import pallas as pl
from jax.experimental.pallas import tpu as pltpu
from jax.sharding import PartitionSpec as P

loss_scale = 1048576.0
clip_norm = 0.004
beta_one = 0.9
beta_two = 0.95
learn_rate = 0.001
weight_decay = 0.1
adam_eps = 1e-08


def project(block_rows, weight_rows):
    return lax.dot_general(
        block_rows, weight_rows, (((1,), (1,)), ((), ())), preferred_element_type=jnp.float32
    )


def plain_body(
    hidden_states, master, moment, second, targets, loss_mask, prior_lse, prior_target, span_order
):
    tok_rows, feat_dim = hidden_states.shape
    shard_rows = master.shape[0]
    ctx_count = lax.axis_size("ctx")
    vocab_count = lax.axis_size("vocab")
    ctx_place = lax.axis_index("ctx")
    vocab_place = lax.axis_index("vocab")
    half_rows = tok_rows // 2
    group_rows = shard_rows * ctx_count
    block_total = group_rows * vocab_count
    head_rows = master.astype(jnp.bfloat16)
    all_targets, all_mask, all_prior, all_outside = (
        lax.all_gather(targets, "ctx", axis=0, tiled=True),
        lax.all_gather(loss_mask, "ctx", axis=0, tiled=True),
        lax.all_gather(prior_lse, "ctx", axis=0, tiled=True),
        lax.all_gather(prior_target, "ctx", axis=0, tiled=True),
    )

    def own_rows(whole):
        pieces = [
            lax.dynamic_slice_in_dim(
                whole, span_order[2 * ctx_place + offset] * half_rows, half_rows, 0
            )
            for offset in (0, 1)
        ]
        return jnp.concatenate(pieces, 0)

    tgt_rows = own_rows(all_targets)
    mask_rows = own_rows(all_mask).astype(jnp.float32)
    prior_rows = own_rows(all_prior)
    outside = own_rows(all_outside)
    local_col = tgt_rows - block_total - vocab_place * group_rows
    token_count = jnp.sum(all_mask.astype(jnp.float32))

    def hit_table(col_count):
        columns = jnp.arange(col_count, dtype=jnp.int32)
        return columns[None, :] == local_col[:, None]

    initial = (
        prior_rows,
        jnp.zeros((tok_rows,), jnp.float32),
        jnp.zeros((tok_rows,), jnp.float32),
        jnp.zeros((tok_rows, group_rows), jnp.float32),
    )
    weight_rows = lax.all_gather(head_rows, "ctx", axis=0, tiled=True)
    block_logits = project(hidden_states, weight_rows)
    new_top = jnp.maximum(initial[0], jnp.max(block_logits, axis=1))
    new_sum = initial[1] * jnp.exp(initial[0] - new_top) + jnp.sum(
        jnp.exp(block_logits - new_top[:, None]), axis=1
    )
    new_target = jnp.sum(jnp.where(hit_table(weight_rows.shape[0]), block_logits, 0.0), axis=1)
    top_value = lax.pmax(new_top, "vocab")
    sum_total, target_sum = lax.psum((new_sum * jnp.exp(new_top - top_value), new_target), "vocab")
    log_total = top_value + jnp.log(jnp.exp(prior_rows - top_value) + sum_total)
    target_logit = jnp.where(tgt_rows >= block_total, target_sum, outside)
    loss_rows = mask_rows * (log_total - target_logit)
    grad_scale = loss_scale / token_count
    onehot = hit_table(group_rows).astype(jnp.float32)
    dlogits = (
        mask_rows[:, None] * (jnp.exp(block_logits - log_total[:, None]) - onehot) * grad_scale
    ).astype(jnp.bfloat16)
    columns = dlogits
    row_grad = lax.psum_scatter(
        lax.dot_general(
            columns, hidden_states, (((0,), (0,)), ((), ())), preferred_element_type=jnp.float32
        ),
        "ctx",
        scatter_dimension=0,
        tiled=True,
    )
    columns = dlogits
    partial_value = jnp.dot(
        columns,
        lax.all_gather(head_rows, "ctx", axis=0, tiled=True),
        preferred_element_type=jnp.float32,
    )
    hidden_grad = lax.psum_scatter(
        partial_value.astype(jnp.bfloat16), "vocab", scatter_dimension=1, tiled=True
    )
    all_losses = lax.all_gather(loss_rows, "ctx", axis=0, tiled=True)
    mean_loss = jnp.sum(all_losses) / token_count
    slot_ids = jnp.arange(span_order.shape[0], dtype=jnp.int32)
    natural = []
    for offset in (0, 1):
        span_id = 2 * ctx_place + offset
        slot_place = jnp.sum(jnp.where(span_order == span_id, slot_ids, 0))
        natural.append(lax.dynamic_slice_in_dim(all_losses, slot_place * half_rows, half_rows, 0))
    token_loss = jnp.concatenate(natural, 0)
    square_sum = lax.psum(jnp.sum(row_grad * row_grad), ("ctx", "vocab"))
    norm_value = jnp.sqrt(square_sum) / loss_scale
    clip_factor = jnp.minimum(1.0, clip_norm / (norm_value + 1e-06))
    clipped = row_grad * clip_factor
    new_moment = beta_one * moment + (1.0 - beta_one) * clipped
    new_second = beta_two * second + (1.0 - beta_two) * clipped * clipped
    new_master = master - learn_rate * (
        new_moment / (jnp.sqrt(new_second) + adam_eps) + weight_decay * master
    )
    return (token_loss, mean_loss, hidden_grad, new_master, new_moment, new_second)


MESH = pl.DeviceIdType.MESH
PLANE = 8
SITES = 4
FOLD = 16
CHUNKS = 4


def fits(shape):
    count = shape["ctx"]
    return shape["vocab"] == 1 and count >= 2 * PLANE and count & (count - 1) == 0


def log2(value):
    return value.bit_length() - 1


def kernel(
    n, shard_rows, order_ref, stats_ref, mst_ref, mom_ref, sec_ref, hid_hbm,
    tl_ref, ml_ref, hg_hbm, nmst_ref, nmom_ref, nsec_ref,
    hid, hg, fold32, wg, w, lg, dl, dlt, st, lb, sqb, sb0, rb0, acc, sb1, rb1, sb2, rb2, gb,
    hin_sem, hout_sem, zs, zr, ps, pr, bs, br, sts, str_, lbs, lbr, sqs, sqr,
    r0s, r0r, r1s, r1r, r2s, r2r,
):
    f32, bf16 = jnp.float32, jnp.bfloat16
    nz = n // PLANE
    feat = hid.shape[1]
    tok = hid.shape[0]
    half_tok = tok // 2
    pieces = FOLD // shard_rows
    cols = feat // pieces
    cc = feat // CHUNKS
    half_rows = shard_rows * SITES * nz
    group_rows = 2 * half_rows
    me = lax.axis_index("ctx")
    core = lax.rem(me, 2)
    site = lax.rem(lax.div(me, 2), SITES)
    z = lax.div(me, PLANE)
    sib = me + 1 - 2 * core

    def slot(c, s, k):
        return (c * SITES + s) * nz + k

    def back(v, d, m):
        return lax.rem(v - d + m, m)

    def fwd(v, d, m):
        return lax.rem(v + d, m)

    def rcopy(src, dst, ssem, rsem, dev):
        return pltpu.make_async_remote_copy(
            src_ref=src, dst_ref=dst, send_sem=ssem, recv_sem=rsem,
            device_id={"ctx": dev}, device_id_type=MESH,
        )

    def site_dev(d):
        return z * PLANE + fwd(site, d, SITES) * 2 + core

    def z_dev(e):
        return fwd(z, e, nz) * PLANE + site * 2 + core

    barrier = pltpu.get_barrier_semaphore()

    def greet(d, carry):
        pl.semaphore_signal(
            barrier, inc=1, device_id={"ctx": fwd(me, d, n)}, device_id_type=MESH
        )
        return carry

    lax.fori_loop(1, n, greet, 0)

    def hin(c):
        sl = pl.ds(c * cc, cc)
        return pltpu.make_async_copy(hid_hbm.at[:, sl], hid.at[:, sl], hin_sem.at[c])

    for c in range(CHUNKS):
        hin(c).start()

    for p in range(pieces):
        fold32[p * shard_rows:(p + 1) * shard_rows, :] = mst_ref[:, p * cols:(p + 1) * cols]
    own = slot(core, site, z)
    wg[own] = fold32[...].astype(bf16)
    st[me] = stats_ref[...]
    pl.semaphore_wait(barrier, n - 1)

    def spread(buf, ssem, rsem):
        def step(d, carry):
            rcopy(buf.at[me], buf.at[me], ssem.at[d], rsem.at[d], fwd(me, d, n)).start()
            return carry

        lax.fori_loop(1, n, step, 0)

    def spread_recv(buf, ssem, rsem):
        def step(d, carry):
            src = back(me, d, n)
            rcopy(buf.at[src], buf.at[src], ssem.at[d], rsem.at[d], src).wait_recv()
            return carry

        lax.fori_loop(1, n, step, 0)

    def spread_sent(buf, ssem, rsem):
        def step(d, carry):
            rcopy(buf.at[me], buf.at[me], ssem.at[d], rsem.at[d], fwd(me, d, n)).wait_send()
            return carry

        lax.fori_loop(1, n, step, 0)

    def zcopy(e, k):
        ref = wg.at[slot(core, site, k)]
        return rcopy(ref, ref, zs.at[e], zr.at[e], z_dev(e))

    def pcopy(e, d, s):
        ref = wg.at[slot(core, s, back(z, e, nz))]
        return rcopy(ref, ref, ps.at[e, d], pr.at[e, d], site_dev(d))

    def bcopy(e, d, c):
        ref = wg.at[slot(c, back(site, d, SITES), back(z, e, nz))]
        return rcopy(ref, ref, bs.at[e, d], br.at[e, d], sib)

    for d in range(1, SITES):
        pcopy(0, d, site).start()
    for e in range(1, nz):
        zcopy(e, z).start()
    bcopy(0, 0, core).start()
    spread(st, sts, str_)
    for e in range(1, nz):
        zcopy(e, back(z, e, nz)).wait_recv()
        for d in range(1, SITES):
            pcopy(e, d, site).start()
        bcopy(e, 0, core).start()
    for e in range(nz):
        for d in range(1, SITES):
            pcopy(e, d, back(site, d, SITES)).wait_recv()
            bcopy(e, d, core).start()

    for c in range(CHUNKS):
        hin(c).wait()

    rb, pb = log2(shard_rows), log2(FOLD)
    tile = min(512, cols)

    def unfold(h):
        orow = lax.broadcasted_iota(jnp.int32, (half_rows, FOLD * SITES * nz), 0)
        icol = lax.broadcasted_iota(jnp.int32, (half_rows, FOLD * SITES * nz), 1)
        base = ((orow >> rb) << pb) + (orow & (shard_rows - 1))
        for p in range(pieces):
            pick = (icol == base + p * shard_rows).astype(f32).astype(bf16)

            def step(t, carry):
                at = pl.multiple_of(t * tile, tile)
                got = wg[pl.ds(h * SITES * nz, SITES * nz), :, pl.ds(at, tile)]
                got = got.reshape(SITES * nz * FOLD, tile)
                out = jnp.dot(pick, got, preferred_element_type=f32).astype(bf16)
                w[h, :, pl.ds(pl.multiple_of(p * cols + at, tile), tile)] = out
                return carry

            lax.fori_loop(0, cols // tile, step, 0)

        def lstep(t, total):
            sl = pl.ds(pl.multiple_of(t * 1024, 1024), 1024)
            return total + lax.dot_general(
                w[h, :, sl], hid[:, sl], (((1,), (1,)), ((), ())), preferred_element_type=f32
            )

        lg[h] = lax.fori_loop(0, feat // 1024, lstep, jnp.zeros((half_rows, tok), f32))

    unfold(core)
    for e in range(nz):
        for d in range(SITES):
            bcopy(e, d, 1 - core).wait_recv()
    unfold(1 - core)

    spread_recv(st, sts, str_)
    picked = []
    for off in range(2):
        span = order_ref[2 * me + off]
        slab = st[lax.div(span, 2)]
        odd = lax.rem(span, 2)
        picked.append(
            [jnp.where(odd == 0, slab[2 * q:2 * q + 1], slab[2 * q + 1:2 * q + 2]) for q in range(4)]
        )
    tgt, mask, prior, outside = [
        jnp.concatenate([picked[0][q], picked[1][q]], axis=1) for q in range(4)
    ]
    token_count = jnp.sum(jnp.sum(st[...], axis=0)[2:4])
    logits = jnp.concatenate([lg[0], lg[1]], axis=0)
    col = lax.broadcasted_iota(jnp.int32, (group_rows, tok), 0)
    place = col >> rb
    zb = log2(nz)
    home = (place & (nz - 1)) * PLANE + ((place >> zb) & (SITES - 1)) * 2 + (place >> (zb + 2))
    natural = home * shard_rows + (col & (shard_rows - 1))
    onehot = (natural.astype(f32) == tgt - float(group_rows)).astype(f32)
    inside = jnp.sum(logits * onehot, axis=0, keepdims=True)
    top = jnp.maximum(prior, jnp.max(logits, axis=0, keepdims=True))
    total = jnp.exp(prior - top) + jnp.sum(jnp.exp(logits - top), axis=0, keepdims=True)
    log_total = top + jnp.log(total)
    target_logit = jnp.where(tgt >= float(group_rows), inside, outside)
    loss = mask * (log_total - target_logit)
    lb[me] = jnp.concatenate(
        [loss[:, :half_tok], loss[:, half_tok:], jnp.zeros((6, half_tok), f32)], axis=0
    )
    spread(lb, lbs, lbr)
    scale = loss_scale / jnp.full((1, 1), token_count, f32)
    dlog = mask * (jnp.exp(logits - log_total) - onehot) * scale
    dl[0] = dlog[:half_rows].astype(bf16)
    dl[1] = dlog[half_rows:].astype(bf16)
    dlt[...] = dlog.T.astype(bf16)

    sub = min(512, cc)

    def grad(h, c, t):
        sl = pl.ds(pl.multiple_of(c * cc + t * sub, sub), sub)
        return jnp.dot(dl[h], hid[:, sl], preferred_element_type=f32)

    def tl(t):
        return pl.ds(pl.multiple_of(t * sub, sub), sub)

    def r0(c):
        return rcopy(sb0.at[c], rb0.at[c], r0s.at[c], r0r.at[c], sib)

    def r1(c, d):
        return rcopy(
            sb1.at[c, fwd(site, d, SITES)], rb1.at[c, d], r1s.at[c, d], r1r.at[c, d], site_dev(d)
        )

    def r2(c, e):
        return rcopy(sb2.at[c, fwd(z, e, nz)], rb2.at[c, e], r2s.at[c, e], r2r.at[c, e], z_dev(e))

    for c in range(CHUNKS):
        def far(t, carry):
            sb0[c, :, tl(t)] = grad(1 - core, c, t).astype(bf16)
            return carry

        lax.fori_loop(0, cc // sub, far, 0)
        r0(c).start()
    for c in range(CHUNKS):
        r0(c).wait_recv()

        def near(t, carry):
            both = grad(core, c, t) + rb0[c, :, tl(t)].astype(f32)
            both = both.reshape(SITES, half_rows // SITES, sub)
            acc[c, :, :, tl(t)] = both
            sb1[c, :, :, tl(t)] = both.astype(bf16)
            return carry

        lax.fori_loop(0, cc // sub, near, 0)
        for d in range(1, SITES):
            r1(c, d).start()

    def hout(c):
        sl = pl.ds(c * cc, cc)
        return pltpu.make_async_copy(hg.at[:, sl], hg_hbm.at[:, sl], hout_sem.at[c])

    for c in range(CHUNKS):
        def back_hidden(t, carry):
            sl = pl.ds(pl.multiple_of(c * cc + t * sub, sub), sub)
            rows = jnp.concatenate([w[0, :, sl], w[1, :, sl]], axis=0)
            hg[:, sl] = jnp.dot(dlt[...], rows, preferred_element_type=f32).astype(bf16)
            return carry

        lax.fori_loop(0, cc // sub, back_hidden, 0)
        hout(c).start()
        for d in range(1, SITES):
            r1(c, d).wait_recv()
        both = acc[c, site]
        for d in range(1, SITES):
            both = both + rb1[c, d].astype(f32)
        for k in range(nz):
            sb2[c, k] = both[k * shard_rows:(k + 1) * shard_rows]
        for e in range(1, nz):
            r2(c, e).start()
    squares = jnp.zeros((shard_rows, cc), f32)
    for c in range(CHUNKS):
        g = sb2[c, z]
        for e in range(1, nz):
            r2(c, e).wait_recv()
            g = g + rb2[c, e]
        gb[:, c * cc:(c + 1) * cc] = g
        squares = squares + g * g
    sqb[me] = jnp.full((8, 128), jnp.sum(squares), f32)
    spread(sqb, sqs, sqr)

    spread_recv(lb, lbs, lbr)
    ml_ref[...] = jnp.full((1, 1), jnp.sum(lb[...]) / token_count, f32)

    def find(j, carry):
        here = order_ref[j]
        a, b = carry
        return (
            jnp.where(here == 2 * me, j, a), jnp.where(here == 2 * me + 1, j, b)
        )

    places = lax.fori_loop(0, 2 * n, find, (jnp.int32(0), jnp.int32(0)))
    for off in range(2):
        slab = lb[lax.div(places[off], 2)]
        odd = lax.rem(places[off], 2)
        tl_ref[off:off + 1, :] = jnp.where(odd == 0, slab[0:1], slab[1:2])

    spread_recv(sqb, sqs, sqr)
    norm = jnp.sqrt(jnp.sum(sqb[...], axis=0)[0:1, 0:1]) / loss_scale
    clip = jnp.minimum(1.0, clip_norm / (norm + 1e-06))

    def adam(t, carry):
        sl = pl.ds(pl.multiple_of(t * 1024, 1024), 1024)
        clipped = gb[:, sl] * clip
        m = beta_one * mom_ref[:, sl] + (1.0 - beta_one) * clipped
        v = beta_two * sec_ref[:, sl] + (1.0 - beta_two) * clipped * clipped
        x = mst_ref[:, sl]
        nmom_ref[:, sl] = m
        nsec_ref[:, sl] = v
        nmst_ref[:, sl] = x - learn_rate * (m / (jnp.sqrt(v) + adam_eps) + weight_decay * x)
        return carry

    lax.fori_loop(0, feat // 1024, adam, 0)

    spread_sent(st, sts, str_)
    spread_sent(lb, lbs, lbr)
    spread_sent(sqb, sqs, sqr)
    for e in range(1, nz):
        zcopy(e, z).wait_send()
    for e in range(nz):
        for d in range(SITES):
            if d:
                pcopy(e, d, site).wait_send()
            bcopy(e, d, core).wait_send()
    for c in range(CHUNKS):
        r0(c).wait_send()
        for d in range(1, SITES):
            r1(c, d).wait_send()
        for e in range(1, nz):
            r2(c, e).wait_send()
        hout(c).wait()


def fused_body(
    hidden_states, master, moment, second, targets, loss_mask, prior_lse, prior_target, span_order
):
    f32, bf16 = jnp.float32, jnp.bfloat16
    tok, feat = hidden_states.shape
    shard_rows = master.shape[0]
    n = lax.axis_size("ctx")
    nz = n // PLANE
    half_tok = tok // 2
    half_rows = shard_rows * SITES * nz
    cc = feat // CHUNKS
    stats = jnp.concatenate(
        [v.astype(f32).reshape(2, half_tok) for v in (targets, loss_mask, prior_lse, prior_target)], 0
    )
    dma = pltpu.SemaphoreType.DMA
    vmem = pl.BlockSpec(memory_space=pltpu.VMEM)
    smem = pl.BlockSpec(memory_space=pltpu.SMEM)
    anyw = pl.BlockSpec(memory_space=pl.ANY)
    out = pl.pallas_call(
        functools.partial(kernel, n, shard_rows),
        out_shape=(
            jax.ShapeDtypeStruct((2, half_tok), f32),
            jax.ShapeDtypeStruct((1, 1), f32),
            jax.ShapeDtypeStruct((tok, feat), bf16),
            jax.ShapeDtypeStruct(master.shape, f32),
            jax.ShapeDtypeStruct(master.shape, f32),
            jax.ShapeDtypeStruct(master.shape, f32),
        ),
        in_specs=[smem, vmem, vmem, vmem, vmem, anyw],
        out_specs=(vmem, vmem, anyw, vmem, vmem, vmem),
        scratch_shapes=[
            pltpu.VMEM((tok, feat), bf16),
            pltpu.VMEM((tok, feat), bf16),
            pltpu.VMEM((FOLD, feat * shard_rows // FOLD), f32),
            pltpu.VMEM((n, FOLD, feat * shard_rows // FOLD), bf16),
            pltpu.VMEM((2, half_rows, feat), bf16),
            pltpu.VMEM((2, half_rows, tok), f32),
            pltpu.VMEM((2, half_rows, tok), bf16),
            pltpu.VMEM((tok, 2 * half_rows), bf16),
            pltpu.VMEM((n, 8, half_tok), f32),
            pltpu.VMEM((n, 8, half_tok), f32),
            pltpu.VMEM((n, 8, 128), f32),
            pltpu.VMEM((CHUNKS, half_rows, cc), bf16),
            pltpu.VMEM((CHUNKS, half_rows, cc), bf16),
            pltpu.VMEM((CHUNKS, SITES, half_rows // SITES, cc), f32),
            pltpu.VMEM((CHUNKS, SITES, half_rows // SITES, cc), bf16),
            pltpu.VMEM((CHUNKS, SITES, half_rows // SITES, cc), bf16),
            pltpu.VMEM((CHUNKS, nz, shard_rows, cc), f32),
            pltpu.VMEM((CHUNKS, nz, shard_rows, cc), f32),
            pltpu.VMEM((shard_rows, feat), f32),
            dma((CHUNKS,)), dma((CHUNKS,)),
            dma((nz,)), dma((nz,)),
            dma((nz, SITES)), dma((nz, SITES)),
            dma((nz, SITES)), dma((nz, SITES)),
            dma((n,)), dma((n,)), dma((n,)), dma((n,)), dma((n,)), dma((n,)),
            dma((CHUNKS,)), dma((CHUNKS,)),
            dma((CHUNKS, SITES)), dma((CHUNKS, SITES)),
            dma((CHUNKS, nz)), dma((CHUNKS, nz)),
        ],
        compiler_params=pltpu.CompilerParams(
            collective_id=0, has_side_effects=True, vmem_limit_bytes=48 * 1024 * 1024
        ),
    )(span_order, stats, master, moment, second, hidden_states)
    token_loss, mean_loss, hidden_grad, new_master, new_moment, new_second = out
    return (
        token_loss.reshape(tok), mean_loss.reshape(()), hidden_grad,
        new_master, new_moment, new_second,
    )


def solution(mesh):
    in_specs = (
        P("ctx", None),
        P(("vocab", "ctx"), None),
        P(("vocab", "ctx"), None),
        P(("vocab", "ctx"), None),
        P("ctx"),
        P("ctx"),
        P("ctx"),
        P("ctx"),
        P(),
    )
    out_specs = (
        P("ctx"),
        P(),
        P("ctx", "vocab"),
        P(("vocab", "ctx"), None),
        P(("vocab", "ctx"), None),
        P(("vocab", "ctx"), None),
    )
    shape = dict(mesh.shape)
    body = fused_body if fits(shape) else plain_body
    return jax.shard_map(body, mesh=mesh, in_specs=in_specs, out_specs=out_specs, check_vma=False)
```

```python
import functools

import jax
import jax.numpy as jnp
from jax import lax
from jax.experimental import pallas as pl
from jax.experimental.pallas import tpu as pltpu
from jax.sharding import PartitionSpec as P

loss_scale = 1048576.0
clip_norm = 0.004
beta_one = 0.9
beta_two = 0.95
learn_rate = 0.001
weight_decay = 0.1
adam_eps = 1e-08


def project(block_rows, weight_rows):
    return lax.dot_general(
        block_rows, weight_rows, (((1,), (1,)), ((), ())), preferred_element_type=jnp.float32
    )


def plain_body(
    hidden_states, master, moment, second, targets, loss_mask, prior_lse, prior_target, span_order
):
    tok_rows, feat_dim = hidden_states.shape
    shard_rows = master.shape[0]
    ctx_count = lax.axis_size("ctx")
    vocab_count = lax.axis_size("vocab")
    ctx_place = lax.axis_index("ctx")
    vocab_place = lax.axis_index("vocab")
    half_rows = tok_rows // 2
    group_rows = shard_rows * ctx_count
    block_total = group_rows * vocab_count
    head_rows = master.astype(jnp.bfloat16)
    all_targets, all_mask, all_prior, all_outside = (
        lax.all_gather(targets, "ctx", axis=0, tiled=True),
        lax.all_gather(loss_mask, "ctx", axis=0, tiled=True),
        lax.all_gather(prior_lse, "ctx", axis=0, tiled=True),
        lax.all_gather(prior_target, "ctx", axis=0, tiled=True),
    )

    def own_rows(whole):
        pieces = [
            lax.dynamic_slice_in_dim(
                whole, span_order[2 * ctx_place + offset] * half_rows, half_rows, 0
            )
            for offset in (0, 1)
        ]
        return jnp.concatenate(pieces, 0)

    tgt_rows = own_rows(all_targets)
    mask_rows = own_rows(all_mask).astype(jnp.float32)
    prior_rows = own_rows(all_prior)
    outside = own_rows(all_outside)
    local_col = tgt_rows - block_total - vocab_place * group_rows
    token_count = jnp.sum(all_mask.astype(jnp.float32))

    def hit_table(col_count):
        columns = jnp.arange(col_count, dtype=jnp.int32)
        return columns[None, :] == local_col[:, None]

    initial = (
        prior_rows,
        jnp.zeros((tok_rows,), jnp.float32),
        jnp.zeros((tok_rows,), jnp.float32),
        jnp.zeros((tok_rows, group_rows), jnp.float32),
    )
    weight_rows = lax.all_gather(head_rows, "ctx", axis=0, tiled=True)
    block_logits = project(hidden_states, weight_rows)
    new_top = jnp.maximum(initial[0], jnp.max(block_logits, axis=1))
    new_sum = initial[1] * jnp.exp(initial[0] - new_top) + jnp.sum(
        jnp.exp(block_logits - new_top[:, None]), axis=1
    )
    new_target = jnp.sum(jnp.where(hit_table(weight_rows.shape[0]), block_logits, 0.0), axis=1)
    top_value = lax.pmax(new_top, "vocab")
    sum_total, target_sum = lax.psum((new_sum * jnp.exp(new_top - top_value), new_target), "vocab")
    log_total = top_value + jnp.log(jnp.exp(prior_rows - top_value) + sum_total)
    target_logit = jnp.where(tgt_rows >= block_total, target_sum, outside)
    loss_rows = mask_rows * (log_total - target_logit)
    grad_scale = loss_scale / token_count
    onehot = hit_table(group_rows).astype(jnp.float32)
    dlogits = (
        mask_rows[:, None] * (jnp.exp(block_logits - log_total[:, None]) - onehot) * grad_scale
    ).astype(jnp.bfloat16)
    columns = dlogits
    row_grad = lax.psum_scatter(
        lax.dot_general(
            columns, hidden_states, (((0,), (0,)), ((), ())), preferred_element_type=jnp.float32
        ),
        "ctx",
        scatter_dimension=0,
        tiled=True,
    )
    columns = dlogits
    partial_value = jnp.dot(
        columns,
        lax.all_gather(head_rows, "ctx", axis=0, tiled=True),
        preferred_element_type=jnp.float32,
    )
    hidden_grad = lax.psum_scatter(
        partial_value.astype(jnp.bfloat16), "vocab", scatter_dimension=1, tiled=True
    )
    all_losses = lax.all_gather(loss_rows, "ctx", axis=0, tiled=True)
    mean_loss = jnp.sum(all_losses) / token_count
    slot_ids = jnp.arange(span_order.shape[0], dtype=jnp.int32)
    natural = []
    for offset in (0, 1):
        span_id = 2 * ctx_place + offset
        slot_place = jnp.sum(jnp.where(span_order == span_id, slot_ids, 0))
        natural.append(lax.dynamic_slice_in_dim(all_losses, slot_place * half_rows, half_rows, 0))
    token_loss = jnp.concatenate(natural, 0)
    square_sum = lax.psum(jnp.sum(row_grad * row_grad), ("ctx", "vocab"))
    norm_value = jnp.sqrt(square_sum) / loss_scale
    clip_factor = jnp.minimum(1.0, clip_norm / (norm_value + 1e-06))
    clipped = row_grad * clip_factor
    new_moment = beta_one * moment + (1.0 - beta_one) * clipped
    new_second = beta_two * second + (1.0 - beta_two) * clipped * clipped
    new_master = master - learn_rate * (
        new_moment / (jnp.sqrt(new_second) + adam_eps) + weight_decay * master
    )
    return (token_loss, mean_loss, hidden_grad, new_master, new_moment, new_second)


MESH = pl.DeviceIdType.MESH
PLANE = 8
SITES = 4
FOLD = 16
CHUNKS = 4
PARTS = 2


def fits(shape):
    count = shape["ctx"]
    return shape["vocab"] == 1 and count >= 2 * PLANE and count & (count - 1) == 0


def log2(value):
    return value.bit_length() - 1


def kernel(
    n, shard_rows, order_hbm, stats_ref, mst_hbm, hid_hbm,
    tl_ref, ml_ref, w, dlt, gb, sq_ref,
    order_ref, mst_ref, hid, fold32, wg, lg, dl, st, lb, sqb, sb0, rb0, acc, sb1, rb1, sb2, rb2,
    in_sem, hin_sem, zs, zr, ps, pr, bs, br, sts, str_, lbs, lbr, sqs, sqr,
    r0s, r0r, r1s, r1r, r2s, r2r,
):
    f32, bf16 = jnp.float32, jnp.bfloat16
    nz = n // PLANE
    feat = hid.shape[1]
    tok = hid.shape[0]
    half_tok = tok // 2
    pieces = FOLD // shard_rows
    cols = feat // pieces
    cc = feat // CHUNKS
    gc = cols // PARTS
    half_rows = shard_rows * SITES * nz
    group_rows = 2 * half_rows
    me = lax.axis_index("ctx")
    core = lax.rem(me, 2)
    site = lax.rem(lax.div(me, 2), SITES)
    z = lax.div(me, PLANE)
    sib = me + 1 - 2 * core

    def slot(c, s, k):
        return (c * SITES + s) * nz + k

    def back(v, d, m):
        return lax.rem(v - d + m, m)

    def fwd(v, d, m):
        return lax.rem(v + d, m)

    def rcopy(src, dst, ssem, rsem, dev):
        return pltpu.make_async_remote_copy(
            src_ref=src, dst_ref=dst, send_sem=ssem, recv_sem=rsem,
            device_id={"ctx": dev}, device_id_type=MESH,
        )

    def site_dev(d):
        return z * PLANE + fwd(site, d, SITES) * 2 + core

    def z_dev(e):
        return fwd(z, e, nz) * PLANE + site * 2 + core

    barrier = pltpu.get_barrier_semaphore()

    def greet(d, carry):
        pl.semaphore_signal(
            barrier, inc=1, device_id={"ctx": fwd(me, d, n)}, device_id_type=MESH
        )
        return carry

    lax.fori_loop(1, n, greet, 0)

    def hin(c):
        sl = pl.ds(c * cc, cc)
        return pltpu.make_async_copy(hid_hbm.at[:, sl], hid.at[:, sl], hin_sem.at[c])

    mst_in = pltpu.make_async_copy(mst_hbm, mst_ref, in_sem.at[0])
    order_in = pltpu.make_async_copy(order_hbm, order_ref, in_sem.at[1])
    mst_in.start()
    order_in.start()
    for c in range(CHUNKS):
        hin(c).start()
    mst_in.wait()

    for p in range(pieces):
        fold32[p * shard_rows:(p + 1) * shard_rows, :] = mst_ref[:, p * cols:(p + 1) * cols]
    own = slot(core, site, z)
    for g in range(PARTS):
        wg[g, own] = fold32[:, g * gc:(g + 1) * gc].astype(bf16)
    st[me] = stats_ref[...]
    pl.semaphore_wait(barrier, n - 1)

    def spread(buf, ssem, rsem):
        def step(d, carry):
            rcopy(buf.at[me], buf.at[me], ssem.at[d], rsem.at[d], fwd(me, d, n)).start()
            return carry

        lax.fori_loop(1, n, step, 0)

    def spread_recv(buf, ssem, rsem):
        def step(d, carry):
            src = back(me, d, n)
            rcopy(buf.at[src], buf.at[src], ssem.at[d], rsem.at[d], src).wait_recv()
            return carry

        lax.fori_loop(1, n, step, 0)

    def spread_sent(buf, ssem, rsem):
        def step(d, carry):
            rcopy(buf.at[me], buf.at[me], ssem.at[d], rsem.at[d], fwd(me, d, n)).wait_send()
            return carry

        lax.fori_loop(1, n, step, 0)

    def zcopy(g, e, k):
        ref = wg.at[g, slot(core, site, k)]
        return rcopy(ref, ref, zs.at[g, e], zr.at[g, e], z_dev(e))

    def pcopy(g, e, d, s):
        ref = wg.at[g, slot(core, s, back(z, e, nz))]
        return rcopy(ref, ref, ps.at[g, e, d], pr.at[g, e, d], site_dev(d))

    def bcopy(g, e, d, c):
        ref = wg.at[g, slot(c, back(site, d, SITES), back(z, e, nz))]
        return rcopy(ref, ref, bs.at[g, e, d], br.at[g, e, d], sib)

    for g in range(PARTS):
        for d in range(1, SITES):
            pcopy(g, 0, d, site).start()
        for e in range(1, nz):
            zcopy(g, e, z).start()
        bcopy(g, 0, 0, core).start()
    spread(st, sts, str_)
    for g in range(PARTS):
        for e in range(1, nz):
            zcopy(g, e, back(z, e, nz)).wait_recv()
            for d in range(1, SITES):
                pcopy(g, e, d, site).start()
            bcopy(g, e, 0, core).start()

    rb, pb = log2(shard_rows), log2(FOLD)
    orow = lax.broadcasted_iota(jnp.int32, (half_rows, FOLD * SITES * nz), 0)
    icol = lax.broadcasted_iota(jnp.int32, (half_rows, FOLD * SITES * nz), 1)
    base = ((orow >> rb) << pb) + (orow & (shard_rows - 1))

    def unfold(g, p):
        pick = (icol == base + p * shard_rows).astype(f32).astype(bf16)
        lo = p * cols + g * gc
        for h in range(2):
            got = wg[g, h * SITES * nz:(h + 1) * SITES * nz]
            got = got.reshape(SITES * nz * FOLD, gc)
            out = jnp.dot(pick, got, preferred_element_type=f32).astype(bf16)
            w[h * half_rows:(h + 1) * half_rows, lo:lo + gc] = out
        part = lax.dot_general(
            w[:, lo:lo + gc], hid[:, lo:lo + gc], (((1,), (1,)), ((), ())),
            preferred_element_type=f32,
        )
        if g == 0 and p == 0:
            lg[...] = part
        else:
            lg[...] += part

    for g in range(PARTS):
        for e in range(nz):
            for d in range(1, SITES):
                pcopy(g, e, d, back(site, d, SITES)).wait_recv()
                bcopy(g, e, d, core).start()
            if g:
                for p in range(e, pieces, nz):
                    unfold(g - 1, p)
        if g == 0:
            for c in range(CHUNKS):
                hin(c).wait()
        for e in range(nz):
            for d in range(SITES):
                bcopy(g, e, d, 1 - core).wait_recv()
    for p in range(pieces):
        unfold(PARTS - 1, p)

    order_in.wait()
    spread_recv(st, sts, str_)
    picked = []
    for off in range(2):
        span = order_ref[2 * me + off]
        slab = st[lax.div(span, 2)]
        odd = lax.rem(span, 2)
        picked.append(
            [jnp.where(odd == 0, slab[2 * q:2 * q + 1], slab[2 * q + 1:2 * q + 2]) for q in range(4)]
        )
    tgt, mask, prior, outside = [
        jnp.concatenate([picked[0][q], picked[1][q]], axis=1) for q in range(4)
    ]
    token_count = jnp.sum(jnp.sum(st[...], axis=0)[2:4])
    logits = lg[...]
    col = lax.broadcasted_iota(jnp.int32, (group_rows, tok), 0)
    place = col >> rb
    zb = log2(nz)
    home = (place & (nz - 1)) * PLANE + ((place >> zb) & (SITES - 1)) * 2 + (place >> (zb + 2))
    natural = home * shard_rows + (col & (shard_rows - 1))
    onehot = (natural.astype(f32) == tgt - float(group_rows)).astype(f32)
    inside = jnp.sum(logits * onehot, axis=0, keepdims=True)
    top = jnp.maximum(prior, jnp.max(logits, axis=0, keepdims=True))
    total = jnp.exp(prior - top) + jnp.sum(jnp.exp(logits - top), axis=0, keepdims=True)
    log_total = top + jnp.log(total)
    target_logit = jnp.where(tgt >= float(group_rows), inside, outside)
    loss = mask * (log_total - target_logit)
    lb[me] = jnp.concatenate(
        [loss[:, :half_tok], loss[:, half_tok:], jnp.zeros((6, half_tok), f32)], axis=0
    )
    spread(lb, lbs, lbr)
    scale = loss_scale / jnp.full((1, 1), token_count, f32)
    dlog = mask * (jnp.exp(logits - log_total) - onehot) * scale
    dl[0] = dlog[:half_rows].astype(bf16)
    dl[1] = dlog[half_rows:].astype(bf16)
    dlt[...] = dlog.T.astype(bf16)

    sub = min(512, cc)

    def grad(h, c, t):
        sl = pl.ds(pl.multiple_of(c * cc + t * sub, sub), sub)
        return jnp.dot(dl[h], hid[:, sl], preferred_element_type=f32)

    def tl(t):
        return pl.ds(pl.multiple_of(t * sub, sub), sub)

    def r0(c):
        return rcopy(sb0.at[c], rb0.at[c], r0s.at[c], r0r.at[c], sib)

    def r1(c, d):
        return rcopy(
            sb1.at[c, fwd(site, d, SITES)], rb1.at[c, d], r1s.at[c, d], r1r.at[c, d], site_dev(d)
        )

    def r2(c, e):
        return rcopy(sb2.at[c, fwd(z, e, nz)], rb2.at[c, e], r2s.at[c, e], r2r.at[c, e], z_dev(e))

    for c in range(CHUNKS):
        def far(t, carry):
            sb0[c, :, tl(t)] = grad(1 - core, c, t).astype(bf16)
            return carry

        lax.fori_loop(0, cc // sub, far, 0)
        r0(c).start()
    for c in range(CHUNKS):
        r0(c).wait_recv()

        def near(t, carry):
            both = grad(core, c, t) + rb0[c, :, tl(t)].astype(f32)
            both = both.reshape(SITES, half_rows // SITES, sub)
            acc[c, :, :, tl(t)] = both
            sb1[c, :, :, tl(t)] = both.astype(bf16)
            return carry

        lax.fori_loop(0, cc // sub, near, 0)
        for d in range(1, SITES):
            r1(c, d).start()

    for c in range(CHUNKS):
        for d in range(1, SITES):
            r1(c, d).wait_recv()
        both = acc[c, site]
        for d in range(1, SITES):
            both = both + rb1[c, d].astype(f32)
        for k in range(nz):
            sb2[c, k] = both[k * shard_rows:(k + 1) * shard_rows]
        for e in range(1, nz):
            r2(c, e).start()
    squares = jnp.zeros((shard_rows, cc), f32)
    for c in range(CHUNKS):
        g = sb2[c, z]
        for e in range(1, nz):
            r2(c, e).wait_recv()
            g = g + rb2[c, e]
        gb[:, c * cc:(c + 1) * cc] = g
        squares = squares + g * g
    sqb[me] = jnp.full((8, 128), jnp.sum(squares), f32)
    spread(sqb, sqs, sqr)

    spread_recv(lb, lbs, lbr)
    ml_ref[...] = jnp.full((1, 1), jnp.sum(lb[...]) / token_count, f32)

    def find(j, carry):
        here = order_ref[j]
        a, b = carry
        return (
            jnp.where(here == 2 * me, j, a), jnp.where(here == 2 * me + 1, j, b)
        )

    places = lax.fori_loop(0, 2 * n, find, (jnp.int32(0), jnp.int32(0)))
    for off in range(2):
        slab = lb[lax.div(places[off], 2)]
        odd = lax.rem(places[off], 2)
        tl_ref[off:off + 1, :] = jnp.where(odd == 0, slab[0:1], slab[1:2])

    spread_recv(sqb, sqs, sqr)
    sq_ref[...] = jnp.sum(sqb[...], axis=0)[0:1, 0:1]

    spread_sent(st, sts, str_)
    spread_sent(lb, lbs, lbr)
    spread_sent(sqb, sqs, sqr)
    for g in range(PARTS):
        for e in range(1, nz):
            zcopy(g, e, z).wait_send()
        for e in range(nz):
            for d in range(SITES):
                if d:
                    pcopy(g, e, d, site).wait_send()
                bcopy(g, e, d, core).wait_send()
    for c in range(CHUNKS):
        r0(c).wait_send()
        for d in range(1, SITES):
            r1(c, d).wait_send()
        for e in range(1, nz):
            r2(c, e).wait_send()


def fused_body(
    hidden_states, master, moment, second, targets, loss_mask, prior_lse, prior_target, span_order
):
    f32, bf16 = jnp.float32, jnp.bfloat16
    tok, feat = hidden_states.shape
    shard_rows = master.shape[0]
    n = lax.axis_size("ctx")
    nz = n // PLANE
    half_tok = tok // 2
    half_rows = shard_rows * SITES * nz
    cc = feat // CHUNKS
    stats = jnp.concatenate(
        [v.astype(f32).reshape(2, half_tok) for v in (targets, loss_mask, prior_lse, prior_target)], 0
    )
    dma = pltpu.SemaphoreType.DMA
    vmem = pl.BlockSpec(memory_space=pltpu.VMEM)
    hbm = pl.BlockSpec(memory_space=pltpu.HBM)
    gc = feat * shard_rows // FOLD // PARTS
    out = pl.pallas_call(
        functools.partial(kernel, n, shard_rows),
        out_shape=(
            jax.ShapeDtypeStruct((2, half_tok), f32),
            jax.ShapeDtypeStruct((1, 1), f32),
            jax.ShapeDtypeStruct((2 * half_rows, feat), bf16),
            jax.ShapeDtypeStruct((tok, 2 * half_rows), bf16),
            jax.ShapeDtypeStruct(master.shape, f32),
            jax.ShapeDtypeStruct((1, 1), f32),
        ),
        in_specs=[hbm, vmem, hbm, hbm],
        out_specs=(vmem, vmem, vmem, vmem, vmem, vmem),
        scratch_shapes=[
            pltpu.SMEM(span_order.shape, jnp.int32),
            pltpu.VMEM(master.shape, f32),
            pltpu.VMEM((tok, feat), bf16),
            pltpu.VMEM((FOLD, feat * shard_rows // FOLD), f32),
            pltpu.VMEM((PARTS, n, FOLD, gc), bf16),
            pltpu.VMEM((2 * half_rows, tok), f32),
            pltpu.VMEM((2, half_rows, tok), bf16),
            pltpu.VMEM((n, 8, half_tok), f32),
            pltpu.VMEM((n, 8, half_tok), f32),
            pltpu.VMEM((n, 8, 128), f32),
            pltpu.VMEM((CHUNKS, half_rows, cc), bf16),
            pltpu.VMEM((CHUNKS, half_rows, cc), bf16),
            pltpu.VMEM((CHUNKS, SITES, half_rows // SITES, cc), f32),
            pltpu.VMEM((CHUNKS, SITES, half_rows // SITES, cc), bf16),
            pltpu.VMEM((CHUNKS, SITES, half_rows // SITES, cc), bf16),
            pltpu.VMEM((CHUNKS, nz, shard_rows, cc), f32),
            pltpu.VMEM((CHUNKS, nz, shard_rows, cc), f32),
            dma((2,)), dma((CHUNKS,)),
            dma((PARTS, nz)), dma((PARTS, nz)),
            dma((PARTS, nz, SITES)), dma((PARTS, nz, SITES)),
            dma((PARTS, nz, SITES)), dma((PARTS, nz, SITES)),
            dma((n,)), dma((n,)), dma((n,)), dma((n,)), dma((n,)), dma((n,)),
            dma((CHUNKS,)), dma((CHUNKS,)),
            dma((CHUNKS, SITES)), dma((CHUNKS, SITES)),
            dma((CHUNKS, nz)), dma((CHUNKS, nz)),
        ],
        compiler_params=pltpu.CompilerParams(
            collective_id=0, has_side_effects=True, vmem_limit_bytes=48 * 1024 * 1024
        ),
    )(span_order, stats, master, hidden_states)
    token_loss, mean_loss, rows, dlogits, row_grad, square_sum = out
    hidden_grad = jnp.dot(dlogits, rows, preferred_element_type=f32).astype(bf16)
    norm_value = jnp.sqrt(square_sum) / loss_scale
    clip_factor = jnp.minimum(1.0, clip_norm / (norm_value + 1e-06))
    clipped = row_grad * clip_factor
    new_moment = beta_one * moment + (1.0 - beta_one) * clipped
    new_second = beta_two * second + (1.0 - beta_two) * clipped * clipped
    new_master = master - learn_rate * (
        new_moment / (jnp.sqrt(new_second) + adam_eps) + weight_decay * master
    )
    return (
        token_loss.reshape(tok), mean_loss.reshape(()), hidden_grad,
        new_master, new_moment, new_second,
    )


def solution(mesh):
    in_specs = (
        P("ctx", None),
        P(("vocab", "ctx"), None),
        P(("vocab", "ctx"), None),
        P(("vocab", "ctx"), None),
        P("ctx"),
        P("ctx"),
        P("ctx"),
        P("ctx"),
        P(),
    )
    out_specs = (
        P("ctx"),
        P(),
        P("ctx", "vocab"),
        P(("vocab", "ctx"), None),
        P(("vocab", "ctx"), None),
        P(("vocab", "ctx"), None),
    )
    shape = dict(mesh.shape)
    body = fused_body if fits(shape) else plain_body
    return jax.shard_map(body, mesh=mesh, in_specs=in_specs, out_specs=out_specs, check_vma=False)
```

```python
import functools

import jax
import jax.numpy as jnp
from jax import lax
from jax.experimental import pallas as pl
from jax.experimental.pallas import tpu as pltpu
from jax.sharding import PartitionSpec as P

loss_scale = 1048576.0
clip_norm = 0.004
beta_one = 0.9
beta_two = 0.95
learn_rate = 0.001
weight_decay = 0.1
adam_eps = 1e-08


def project(block_rows, weight_rows):
    return lax.dot_general(
        block_rows, weight_rows, (((1,), (1,)), ((), ())), preferred_element_type=jnp.float32
    )


def plain_body(
    hidden_states, master, moment, second, targets, loss_mask, prior_lse, prior_target, span_order
):
    tok_rows, feat_dim = hidden_states.shape
    shard_rows = master.shape[0]
    ctx_count = lax.axis_size("ctx")
    vocab_count = lax.axis_size("vocab")
    ctx_place = lax.axis_index("ctx")
    vocab_place = lax.axis_index("vocab")
    half_rows = tok_rows // 2
    group_rows = shard_rows * ctx_count
    block_total = group_rows * vocab_count
    head_rows = master.astype(jnp.bfloat16)
    all_targets, all_mask, all_prior, all_outside = (
        lax.all_gather(targets, "ctx", axis=0, tiled=True),
        lax.all_gather(loss_mask, "ctx", axis=0, tiled=True),
        lax.all_gather(prior_lse, "ctx", axis=0, tiled=True),
        lax.all_gather(prior_target, "ctx", axis=0, tiled=True),
    )

    def own_rows(whole):
        pieces = [
            lax.dynamic_slice_in_dim(
                whole, span_order[2 * ctx_place + offset] * half_rows, half_rows, 0
            )
            for offset in (0, 1)
        ]
        return jnp.concatenate(pieces, 0)

    tgt_rows = own_rows(all_targets)
    mask_rows = own_rows(all_mask).astype(jnp.float32)
    prior_rows = own_rows(all_prior)
    outside = own_rows(all_outside)
    local_col = tgt_rows - block_total - vocab_place * group_rows
    token_count = jnp.sum(all_mask.astype(jnp.float32))

    def hit_table(col_count):
        columns = jnp.arange(col_count, dtype=jnp.int32)
        return columns[None, :] == local_col[:, None]

    initial = (
        prior_rows,
        jnp.zeros((tok_rows,), jnp.float32),
        jnp.zeros((tok_rows,), jnp.float32),
        jnp.zeros((tok_rows, group_rows), jnp.float32),
    )
    weight_rows = lax.all_gather(head_rows, "ctx", axis=0, tiled=True)
    block_logits = project(hidden_states, weight_rows)
    new_top = jnp.maximum(initial[0], jnp.max(block_logits, axis=1))
    new_sum = initial[1] * jnp.exp(initial[0] - new_top) + jnp.sum(
        jnp.exp(block_logits - new_top[:, None]), axis=1
    )
    new_target = jnp.sum(jnp.where(hit_table(weight_rows.shape[0]), block_logits, 0.0), axis=1)
    top_value = lax.pmax(new_top, "vocab")
    sum_total, target_sum = lax.psum((new_sum * jnp.exp(new_top - top_value), new_target), "vocab")
    log_total = top_value + jnp.log(jnp.exp(prior_rows - top_value) + sum_total)
    target_logit = jnp.where(tgt_rows >= block_total, target_sum, outside)
    loss_rows = mask_rows * (log_total - target_logit)
    grad_scale = loss_scale / token_count
    onehot = hit_table(group_rows).astype(jnp.float32)
    dlogits = (
        mask_rows[:, None] * (jnp.exp(block_logits - log_total[:, None]) - onehot) * grad_scale
    ).astype(jnp.bfloat16)
    columns = dlogits
    row_grad = lax.psum_scatter(
        lax.dot_general(
            columns, hidden_states, (((0,), (0,)), ((), ())), preferred_element_type=jnp.float32
        ),
        "ctx",
        scatter_dimension=0,
        tiled=True,
    )
    columns = dlogits
    partial_value = jnp.dot(
        columns,
        lax.all_gather(head_rows, "ctx", axis=0, tiled=True),
        preferred_element_type=jnp.float32,
    )
    hidden_grad = lax.psum_scatter(
        partial_value.astype(jnp.bfloat16), "vocab", scatter_dimension=1, tiled=True
    )
    all_losses = lax.all_gather(loss_rows, "ctx", axis=0, tiled=True)
    mean_loss = jnp.sum(all_losses) / token_count
    slot_ids = jnp.arange(span_order.shape[0], dtype=jnp.int32)
    natural = []
    for offset in (0, 1):
        span_id = 2 * ctx_place + offset
        slot_place = jnp.sum(jnp.where(span_order == span_id, slot_ids, 0))
        natural.append(lax.dynamic_slice_in_dim(all_losses, slot_place * half_rows, half_rows, 0))
    token_loss = jnp.concatenate(natural, 0)
    square_sum = lax.psum(jnp.sum(row_grad * row_grad), ("ctx", "vocab"))
    norm_value = jnp.sqrt(square_sum) / loss_scale
    clip_factor = jnp.minimum(1.0, clip_norm / (norm_value + 1e-06))
    clipped = row_grad * clip_factor
    new_moment = beta_one * moment + (1.0 - beta_one) * clipped
    new_second = beta_two * second + (1.0 - beta_two) * clipped * clipped
    new_master = master - learn_rate * (
        new_moment / (jnp.sqrt(new_second) + adam_eps) + weight_decay * master
    )
    return (token_loss, mean_loss, hidden_grad, new_master, new_moment, new_second)


MESH = pl.DeviceIdType.MESH
PLANE = 8
SITES = 4
FOLD = 16
CHUNKS = 8
PARTS = 2


def fits(shape):
    count = shape["ctx"]
    return shape["vocab"] == 1 and count >= 2 * PLANE and count & (count - 1) == 0


def log2(value):
    return value.bit_length() - 1


def kernel(
    n, shard_rows, order_hbm, stats_ref, mst_hbm, hid_hbm,
    tl_ref, ml_ref, w, dlt, gb, sq_ref,
    order_ref, mst_ref, hid, fold32, wg, lg, dl, st, lb, sqa, sqb, sb0, rb0, acc, sb1, rb1, sb2, rb2,
    in_sem, hin_sem, zs, zr, ps, pr, bs, br, st_sem, lb_sem, sq_sem,
    r0s, r0r, r1s, r1r, r2s, r2r,
):
    f32, bf16 = jnp.float32, jnp.bfloat16
    nz = n // PLANE
    feat = hid.shape[1]
    tok = hid.shape[0]
    half_tok = tok // 2
    pieces = FOLD // shard_rows
    cols = feat // pieces
    cc = feat // CHUNKS
    gc = cols // PARTS
    half_rows = shard_rows * SITES * nz
    group_rows = 2 * half_rows
    me = lax.axis_index("ctx")
    core = lax.rem(me, 2)
    site = lax.rem(lax.div(me, 2), SITES)
    z = lax.div(me, PLANE)
    sib = me + 1 - 2 * core

    def slot(c, s, k):
        return (c * SITES + s) * nz + k

    def back(v, d, m):
        return lax.rem(v - d + m, m)

    def fwd(v, d, m):
        return lax.rem(v + d, m)

    def rcopy(src, dst, ssem, rsem, dev):
        return pltpu.make_async_remote_copy(
            src_ref=src, dst_ref=dst, send_sem=ssem, recv_sem=rsem,
            device_id={"ctx": dev}, device_id_type=MESH,
        )

    def site_dev(d):
        return z * PLANE + fwd(site, d, SITES) * 2 + core

    def z_dev(e):
        return fwd(z, e, nz) * PLANE + site * 2 + core

    barrier = pltpu.get_barrier_semaphore()

    partners = [sib] + [site_dev(d) for d in range(1, SITES)] + [z_dev(e) for e in range(1, nz)]
    for dev in partners:
        pl.semaphore_signal(barrier, inc=1, device_id={"ctx": dev}, device_id_type=MESH)

    def hin(c):
        sl = pl.ds(c * cc, cc)
        return pltpu.make_async_copy(hid_hbm.at[:, sl], hid.at[:, sl], hin_sem.at[c])

    mst_in = pltpu.make_async_copy(mst_hbm, mst_ref, in_sem.at[0])
    order_in = pltpu.make_async_copy(order_hbm, order_ref, in_sem.at[1])
    mst_in.start()
    order_in.start()
    for c in range(CHUNKS):
        hin(c).start()
    mst_in.wait()

    for p in range(pieces):
        fold32[p * shard_rows:(p + 1) * shard_rows, :] = mst_ref[:, p * cols:(p + 1) * cols]
    own = slot(core, site, z)
    for g in range(PARTS):
        wg[g, own] = fold32[:, g * gc:(g + 1) * gc].astype(bf16)
    st[own] = stats_ref[...]
    pl.semaphore_wait(barrier, len(partners))

    def zbulk(buf, sems, e, k):
        ref = buf.at[slot(core, site, k)]
        return rcopy(ref, ref, sems.at[0, e], sems.at[1, e], z_dev(e))

    def pbulk(buf, sems, d, s):
        ref = buf.at[pl.ds(slot(core, s, 0), nz)]
        return rcopy(ref, ref, sems.at[0, nz + d], sems.at[1, nz + d], site_dev(d))

    def bbulk(buf, sems, c):
        ref = buf.at[pl.ds(c * SITES * nz, SITES * nz)]
        return rcopy(ref, ref, sems.at[0, 0], sems.at[1, 0], sib)

    def first(buf, sems):
        for e in range(1, nz):
            zbulk(buf, sems, e, z).start()

    def second(buf, sems):
        for e in range(1, nz):
            zbulk(buf, sems, e, back(z, e, nz)).wait_recv()
        for d in range(1, SITES):
            pbulk(buf, sems, d, site).start()

    def third(buf, sems):
        for d in range(1, SITES):
            pbulk(buf, sems, d, back(site, d, SITES)).wait_recv()
        bbulk(buf, sems, core).start()

    def bulk_sent(buf, sems):
        for e in range(1, nz):
            zbulk(buf, sems, e, z).wait_send()
        for d in range(1, SITES):
            pbulk(buf, sems, d, site).wait_send()
        bbulk(buf, sems, core).wait_send()

    def device_slot(dev):
        return slot(lax.rem(dev, 2), lax.rem(lax.div(dev, 2), SITES), lax.div(dev, PLANE))

    def zcopy(g, e, k):
        ref = wg.at[g, slot(core, site, k)]
        return rcopy(ref, ref, zs.at[g, e], zr.at[g, e], z_dev(e))

    def pcopy(g, e, d, s):
        ref = wg.at[g, slot(core, s, back(z, e, nz))]
        return rcopy(ref, ref, ps.at[g, e, d], pr.at[g, e, d], site_dev(d))

    def bcopy(g, e, d, c):
        ref = wg.at[g, slot(c, back(site, d, SITES), back(z, e, nz))]
        return rcopy(ref, ref, bs.at[g, e, d], br.at[g, e, d], sib)

    for g in range(PARTS):
        for d in range(1, SITES):
            pcopy(g, 0, d, site).start()
        for e in range(1, nz):
            zcopy(g, e, z).start()
        bcopy(g, 0, 0, core).start()
    first(st, st_sem)
    for g in range(PARTS):
        if g == PARTS - 1:
            second(st, st_sem)
        for e in range(1, nz):
            zcopy(g, e, back(z, e, nz)).wait_recv()
            for d in range(1, SITES):
                pcopy(g, e, d, site).start()
            bcopy(g, e, 0, core).start()

    rb, pb = log2(shard_rows), log2(FOLD)
    orow = lax.broadcasted_iota(jnp.int32, (half_rows, FOLD * SITES * nz), 0)
    icol = lax.broadcasted_iota(jnp.int32, (half_rows, FOLD * SITES * nz), 1)
    base = ((orow >> rb) << pb) + (orow & (shard_rows - 1))

    def unfold(g, p):
        pick = (icol == base + p * shard_rows).astype(f32).astype(bf16)
        lo = p * cols + g * gc
        for h in range(2):
            got = wg[g, h * SITES * nz:(h + 1) * SITES * nz]
            got = got.reshape(SITES * nz * FOLD, gc)
            out = jnp.dot(pick, got, preferred_element_type=f32).astype(bf16)
            w[h * half_rows:(h + 1) * half_rows, lo:lo + gc] = out
        part = lax.dot_general(
            w[:, lo:lo + gc], hid[:, lo:lo + gc], (((1,), (1,)), ((), ())),
            preferred_element_type=f32,
        )
        if g == 0 and p == 0:
            lg[...] = part
        else:
            lg[...] += part

    for g in range(PARTS):
        for e in range(nz):
            for d in range(1, SITES):
                pcopy(g, e, d, back(site, d, SITES)).wait_recv()
                bcopy(g, e, d, core).start()
            if g:
                for p in range(e, pieces, nz):
                    unfold(g - 1, p)
        if g == 0:
            third(st, st_sem)
            for c in range(CHUNKS):
                hin(c).wait()
        for e in range(nz):
            for d in range(SITES):
                bcopy(g, e, d, 1 - core).wait_recv()
    for p in range(pieces):
        unfold(PARTS - 1, p)

    order_in.wait()
    bbulk(st, st_sem, 1 - core).wait_recv()
    picked = []
    for off in range(2):
        span = order_ref[2 * me + off]
        slab = st[device_slot(lax.div(span, 2))]
        odd = lax.rem(span, 2)
        picked.append(
            [jnp.where(odd == 0, slab[2 * q:2 * q + 1], slab[2 * q + 1:2 * q + 2]) for q in range(4)]
        )
    tgt, mask, prior, outside = [
        jnp.concatenate([picked[0][q], picked[1][q]], axis=1) for q in range(4)
    ]
    token_count = jnp.sum(jnp.sum(st[...], axis=0)[2:4])
    logits = lg[...]
    col = lax.broadcasted_iota(jnp.int32, (group_rows, tok), 0)
    place = col >> rb
    zb = log2(nz)
    home = (place & (nz - 1)) * PLANE + ((place >> zb) & (SITES - 1)) * 2 + (place >> (zb + 2))
    natural = home * shard_rows + (col & (shard_rows - 1))
    onehot = (natural.astype(f32) == tgt - float(group_rows)).astype(f32)
    inside = jnp.sum(logits * onehot, axis=0, keepdims=True)
    top = jnp.maximum(prior, jnp.max(logits, axis=0, keepdims=True))
    total = jnp.exp(prior - top) + jnp.sum(jnp.exp(logits - top), axis=0, keepdims=True)
    log_total = top + jnp.log(total)
    target_logit = jnp.where(tgt >= float(group_rows), inside, outside)
    loss = mask * (log_total - target_logit)
    lb[own] = jnp.concatenate(
        [loss[:, :half_tok], loss[:, half_tok:], jnp.zeros((6, half_tok), f32)], axis=0
    )
    first(lb, lb_sem)
    scale = loss_scale / jnp.full((1, 1), token_count, f32)
    dlog = mask * (jnp.exp(logits - log_total) - onehot) * scale
    dl[0] = dlog[:half_rows].astype(bf16)
    dl[1] = dlog[half_rows:].astype(bf16)
    dlt[...] = dlog.T.astype(bf16)

    sub = min(512, cc)

    def grad(h, c, t):
        sl = pl.ds(pl.multiple_of(c * cc + t * sub, sub), sub)
        return jnp.dot(dl[h], hid[:, sl], preferred_element_type=f32)

    def tl(t):
        return pl.ds(pl.multiple_of(t * sub, sub), sub)

    def r0(c):
        return rcopy(sb0.at[c], rb0.at[c], r0s.at[c], r0r.at[c], sib)

    def r1(c, d):
        return rcopy(
            sb1.at[c, fwd(site, d, SITES)], rb1.at[c, d], r1s.at[c, d], r1r.at[c, d], site_dev(d)
        )

    def r2(c, e):
        return rcopy(sb2.at[c, fwd(z, e, nz)], rb2.at[c, e], r2s.at[c, e], r2r.at[c, e], z_dev(e))

    for c in range(CHUNKS):
        def far(t, carry):
            sb0[c, :, tl(t)] = grad(1 - core, c, t).astype(bf16)
            return carry

        lax.fori_loop(0, cc // sub, far, 0)
        r0(c).start()
    second(lb, lb_sem)
    for c in range(CHUNKS):
        r0(c).wait_recv()

        def near(t, carry):
            both = grad(core, c, t) + rb0[c, :, tl(t)].astype(f32)
            both = both.reshape(SITES, half_rows // SITES, sub)
            acc[c, :, :, tl(t)] = both
            sb1[c, :, :, tl(t)] = both.astype(bf16)
            return carry

        lax.fori_loop(0, cc // sub, near, 0)
        for d in range(1, SITES):
            r1(c, d).start()
    third(lb, lb_sem)

    for c in range(CHUNKS):
        for d in range(1, SITES):
            r1(c, d).wait_recv()
        both = acc[c, site]
        for d in range(1, SITES):
            both = both + rb1[c, d].astype(f32)
        for k in range(nz):
            sb2[c, k] = both[k * shard_rows:(k + 1) * shard_rows]
        for e in range(1, nz):
            r2(c, e).start()
    squares = jnp.zeros((shard_rows, cc), f32)
    for c in range(CHUNKS):
        g = sb2[c, z]
        for e in range(1, nz):
            r2(c, e).wait_recv()
            g = g + rb2[c, e]
        gb[:, c * cc:(c + 1) * cc] = g
        squares = squares + g * g
    def hop(src, dst, dev):
        return rcopy(sqa.at[src], sqb.at[dst], sq_sem.at[0, dst], sq_sem.at[1, dst], dev)

    def hop_sum(value, src, hops):
        sqa[src] = value
        for dst, dev in hops:
            hop(src, dst, dev).start()
        return value, src, hops

    def hop_done(value, src, hops):
        for dst, dev in hops:
            hop(src, dst, dev).wait_recv()
            value = value + sqb[dst]
        return value

    by_core = [(0, sib)]
    by_site = [(d, site_dev(d)) for d in range(1, SITES)]
    by_z = [(SITES - 1 + e, z_dev(e)) for e in range(1, nz)]
    pending = hop_sum(jnp.full((8, 128), jnp.sum(squares), f32), 0, by_core)
    bbulk(lb, lb_sem, 1 - core).wait_recv()
    pending = hop_sum(hop_done(*pending), 1, by_site)
    ml_ref[...] = jnp.full((1, 1), jnp.sum(lb[...]) / token_count, f32)

    def find(j, carry):
        here = order_ref[j]
        a, b = carry
        return (
            jnp.where(here == 2 * me, j, a), jnp.where(here == 2 * me + 1, j, b)
        )

    pending = hop_sum(hop_done(*pending), 2, by_z)
    places = lax.fori_loop(0, 2 * n, find, (jnp.int32(0), jnp.int32(0)))
    for off in range(2):
        slab = lb[device_slot(lax.div(places[off], 2))]
        odd = lax.rem(places[off], 2)
        tl_ref[off:off + 1, :] = jnp.where(odd == 0, slab[0:1], slab[1:2])

    sq_ref[...] = hop_done(*pending)[0:1, 0:1]

    bulk_sent(st, st_sem)
    bulk_sent(lb, lb_sem)
    for src, hops in enumerate((by_core, by_site, by_z)):
        for dst, dev in hops:
            hop(src, dst, dev).wait_send()
    for g in range(PARTS):
        for e in range(1, nz):
            zcopy(g, e, z).wait_send()
        for e in range(nz):
            for d in range(SITES):
                if d:
                    pcopy(g, e, d, site).wait_send()
                bcopy(g, e, d, core).wait_send()
    for c in range(CHUNKS):
        r0(c).wait_send()
        for d in range(1, SITES):
            r1(c, d).wait_send()
        for e in range(1, nz):
            r2(c, e).wait_send()


def fused_body(
    hidden_states, master, moment, second, targets, loss_mask, prior_lse, prior_target, span_order
):
    f32, bf16 = jnp.float32, jnp.bfloat16
    tok, feat = hidden_states.shape
    shard_rows = master.shape[0]
    n = lax.axis_size("ctx")
    nz = n // PLANE
    half_tok = tok // 2
    half_rows = shard_rows * SITES * nz
    cc = feat // CHUNKS
    stats = jnp.concatenate(
        [v.astype(f32).reshape(2, half_tok) for v in (targets, loss_mask, prior_lse, prior_target)], 0
    )
    dma = pltpu.SemaphoreType.DMA
    vmem = pl.BlockSpec(memory_space=pltpu.VMEM)
    hbm = pl.BlockSpec(memory_space=pltpu.HBM)
    gc = feat * shard_rows // FOLD // PARTS
    out = pl.pallas_call(
        functools.partial(kernel, n, shard_rows),
        out_shape=(
            jax.ShapeDtypeStruct((2, half_tok), f32),
            jax.ShapeDtypeStruct((1, 1), f32),
            jax.ShapeDtypeStruct((2 * half_rows, feat), bf16),
            jax.ShapeDtypeStruct((tok, 2 * half_rows), bf16),
            jax.ShapeDtypeStruct(master.shape, f32),
            jax.ShapeDtypeStruct((1, 1), f32),
        ),
        in_specs=[hbm, vmem, hbm, hbm],
        out_specs=(vmem, vmem, vmem, vmem, vmem, vmem),
        scratch_shapes=[
            pltpu.SMEM(span_order.shape, jnp.int32),
            pltpu.VMEM(master.shape, f32),
            pltpu.VMEM((tok, feat), bf16),
            pltpu.VMEM((FOLD, feat * shard_rows // FOLD), f32),
            pltpu.VMEM((PARTS, n, FOLD, gc), bf16),
            pltpu.VMEM((2 * half_rows, tok), f32),
            pltpu.VMEM((2, half_rows, tok), bf16),
            pltpu.VMEM((n, 8, half_tok), f32),
            pltpu.VMEM((n, 8, half_tok), f32),
            pltpu.VMEM((3, 8, 128), f32),
            pltpu.VMEM((SITES + nz, 8, 128), f32),
            pltpu.VMEM((CHUNKS, half_rows, cc), bf16),
            pltpu.VMEM((CHUNKS, half_rows, cc), bf16),
            pltpu.VMEM((CHUNKS, SITES, half_rows // SITES, cc), f32),
            pltpu.VMEM((CHUNKS, SITES, half_rows // SITES, cc), bf16),
            pltpu.VMEM((CHUNKS, SITES, half_rows // SITES, cc), bf16),
            pltpu.VMEM((CHUNKS, nz, shard_rows, cc), f32),
            pltpu.VMEM((CHUNKS, nz, shard_rows, cc), f32),
            dma((2,)), dma((CHUNKS,)),
            dma((PARTS, nz)), dma((PARTS, nz)),
            dma((PARTS, nz, SITES)), dma((PARTS, nz, SITES)),
            dma((PARTS, nz, SITES)), dma((PARTS, nz, SITES)),
            dma((2, nz + SITES)), dma((2, nz + SITES)), dma((2, nz + SITES)),
            dma((CHUNKS,)), dma((CHUNKS,)),
            dma((CHUNKS, SITES)), dma((CHUNKS, SITES)),
            dma((CHUNKS, nz)), dma((CHUNKS, nz)),
        ],
        compiler_params=pltpu.CompilerParams(
            collective_id=0, has_side_effects=True, vmem_limit_bytes=48 * 1024 * 1024
        ),
    )(span_order, stats, master, hidden_states)
    token_loss, mean_loss, rows, dlogits, row_grad, square_sum = out
    hidden_grad = jnp.dot(dlogits, rows, preferred_element_type=f32).astype(bf16)
    norm_value = jnp.sqrt(square_sum) / loss_scale
    clip_factor = jnp.minimum(1.0, clip_norm / (norm_value + 1e-06))
    clipped = row_grad * clip_factor
    new_moment = beta_one * moment + (1.0 - beta_one) * clipped
    new_second = beta_two * second + (1.0 - beta_two) * clipped * clipped
    new_master = master - learn_rate * (
        new_moment / (jnp.sqrt(new_second) + adam_eps) + weight_decay * master
    )
    return (
        token_loss.reshape(tok), mean_loss.reshape(()), hidden_grad,
        new_master, new_moment, new_second,
    )


def solution(mesh):
    in_specs = (
        P("ctx", None),
        P(("vocab", "ctx"), None),
        P(("vocab", "ctx"), None),
        P(("vocab", "ctx"), None),
        P("ctx"),
        P("ctx"),
        P("ctx"),
        P("ctx"),
        P(),
    )
    out_specs = (
        P("ctx"),
        P(),
        P("ctx", "vocab"),
        P(("vocab", "ctx"), None),
        P(("vocab", "ctx"), None),
        P(("vocab", "ctx"), None),
    )
    shape = dict(mesh.shape)
    body = fused_body if fits(shape) else plain_body
    return jax.shard_map(body, mesh=mesh, in_specs=in_specs, out_specs=out_specs, check_vma=False)
```
